32 devices in a mesh: dp: 8 (over z, x), tensor: 4 (over y, core).
Axes of the slice: x: 2, y: 2, z: 4, core: 2. Of those that a mesh axis runs over, the one named last changes fastest.
Arguments:
- tokens: bfloat16 [16384, 1024], P(('dp', 'tensor')), may hold values from -6 to 6
- segments: int32 [16384], P('dp'), may hold values from 0 to 4, as said below
- norm_gains: bfloat16 [2, 1024], P(None, 'dp'), may hold values from 0.099609375 to 1.8984375
- norm_biases: bfloat16 [2, 1024], P(None, 'dp'), may hold values from -3 to 3
- qkv_weight: bfloat16 [1024, 3, 1024], P('dp', None, 'tensor'), may hold values from -0.1875 to 0.1875
- qv_bias: bfloat16 [16, 128], P('tensor', 'dp'), may hold values from -4 to 4
- out_weight: bfloat16 [1024, 1024], P('tensor', 'dp'), may hold values from -0.75 to 0.75
- out_bias: bfloat16 [1024], P('dp'), may hold values from -4 to 4
- up_weight: bfloat16 [1024, 4096], P('dp', 'tensor'), may hold values from -0.1875 to 0.1875
- up_bias: bfloat16 [32, 128], P('tensor', 'dp'), may hold values from -4 to 4
- down_weight: bfloat16 [4096, 1024], P('tensor', 'dp'), may hold values from -0.09375 to 0.09375
- down_bias: bfloat16 [1024], P('dp'), may hold values from -4 to 4
- out_grad: bfloat16 [16384, 1024], P(('dp', 'tensor')), may hold values from -6 to 6
Outputs:
- output: bfloat16 [16384, 1024], P(('dp', 'tensor'))
- input_grad: float32 [16384, 1024], P(('dp', 'tensor'))
- norm_gains_grad: float32 [2, 1024], P(None, 'dp')
- norm_biases_grad: float32 [2, 1024], P(None, 'dp')
- qkv_weight_grad: float32 [1024, 3, 1024], P('dp', None, 'tensor')
- qv_bias_grad: float32 [16, 128], P('tensor', 'dp')
- out_weight_grad: float32 [1024, 1024], P('tensor', 'dp')
- out_bias_grad: float32 [1024], P('dp')
- up_weight_grad: float32 [1024, 4096], P('dp', 'tensor')
- up_bias_grad: float32 [32, 128], P('tensor', 'dp')
- down_weight_grad: float32 [4096, 1024], P('tensor', 'dp')
- down_bias_grad: float32 [1024], P('dp')
The draws below stay inside these ranges and needn't reach their ends.
Inputs may be any that keep to these rules, and one draw needn't show every extreme that they name: `segments`: within each packed sequence of 2048 tokens the document numbers never fall; every sequence holds five documents, numbered from 0.
All inputs are finite; a program needn't handle non-finite values.
Results may differ from the reference program's by a relative error of at most 0.017.
Values may be sent and summed in bfloat16 or wider, within the bound.
A program may use at most 192 MiB of HBM per device.

```python
import jax
import jax.numpy as jnp
from jax import lax

D = 1024
H = 16
HD = 64
FF = 4096
SEQ_LEN = 2048
TOKENS = 16384


def draw_segments(key, part):
    key = jax.random.fold_in(key, 7)
    keys = jax.random.split(key, 4)
    count = TOKENS // SEQ_LEN
    eighth = SEQ_LEN // 8
    first = jax.random.randint(keys[0], (count, 1), 1, eighth)
    second = jax.random.randint(keys[1], (count, 1), eighth, 2 * eighth)
    third = jax.random.randint(keys[2], (count, 1), 6 * eighth + 1, 7 * eighth + 1)
    fourth = jax.random.randint(keys[3], (count, 1), 7 * eighth + 1, 8 * eighth)
    place = jnp.arange(SEQ_LEN, dtype=jnp.int32)[None, :]
    number = (place >= first).astype(jnp.int32) + (place >= second).astype(jnp.int32) + (place >= third).astype(jnp.int32) + (place >= fourth).astype(jnp.int32)
    return number.reshape(TOKENS).astype(jnp.int32)


def with_spikes(entries, key, source, target, blocks, factor):
    def block_of(dim):
        return (jnp.arange(entries.shape[dim]) // (entries.shape[dim] // blocks)).reshape((-1,) + (1,) * (entries.ndim - 1 - dim))

    first = jax.random.permutation(key, blocks)[block_of(target)]
    other_side = (block_of(target) + blocks // 2) % blocks
    return jnp.where((block_of(source) == first) | (block_of(source) == other_side), factor * entries, entries)


def shard_levels(own_key, dims, pieces, smallest, largest):
    def one(position, blocks):
        heights = jax.random.uniform(jax.random.fold_in(jax.random.fold_in(own_key, 6), position), (blocks,), jnp.float32, smallest / len(pieces), largest / len(pieces))
        return jnp.repeat(jnp.exp(heights), dims[position] // blocks).reshape((-1,) + (1,) * (len(dims) - position - 1))

    level = one(*pieces[0])
    for cut in pieces[1:]:
        level = level * one(*cut)
    return level


def scatter_about(rng, shape, scale, bound, cuts=(), kind=jnp.bfloat16):
    level = shard_levels(rng, shape, cuts, -0.22, 0.18) if cuts else 1.0
    array = jax.random.normal(rng, shape, jnp.float32) * scale * level
    return jnp.minimum(jnp.maximum(array, -bound), bound).astype(kind)


def noise_with(stream_key, shape, scale, most, pieces, heavy, held_as=jnp.bfloat16):
    values = scale * jax.random.normal(stream_key, shape, jnp.float32)
    if pieces:
        values = values * shard_levels(stream_key, shape, pieces, -0.22, 0.18)
    return jnp.clip(with_spikes(values, jax.random.fold_in(stream_key, 3), *heavy), -most, most).astype(held_as)


def setup_inputs(seed: int = 0) -> dict:
    streams_of = jax.random.split(jax.random.key(seed), 14)
    return {
        "tokens": scatter_about(streams_of[0], (TOKENS, D), 1.0, 6.0, ((0, 32),)),
        "segments": draw_segments(jax.random.fold_in(streams_of[13], 71), 0),
        "norm_gains": jnp.clip(1.0 + 0.18 * jax.random.normal(streams_of[2], (2, D), jnp.float32), 0.099609375, 1.8984375).astype(jnp.bfloat16),
        "norm_biases": scatter_about(streams_of[3], (2, D), 0.3, 3.0, ((1, 8),)),
        "qkv_weight": scatter_about(streams_of[4], (D, 3, D), D ** -0.5, 0.1875, ((0, 8), (2, 4))),
        "qv_bias": scatter_about(streams_of[5], (H, 2 * HD), 0.5, 4.0, ((0, 4), (1, 8))),
        "out_weight": scatter_about(streams_of[6], (D, D), (D // 16) ** -0.5, 0.75, ((0, 4), (1, 8))),
        "out_bias": scatter_about(streams_of[7], (D,), 0.5, 4.0, ((0, 8),)),
        "up_weight": scatter_about(streams_of[8], (D, FF), D ** -0.5, 0.1875, ((0, 8), (1, 4))),
        "up_bias": scatter_about(streams_of[9], (FF // 128, 128), 0.5, 4.0, ((0, 4), (1, 8))),
        "down_weight": scatter_about(streams_of[10], (FF, D), FF ** -0.5, 0.09375, ((0, 4), (1, 8))),
        "down_bias": scatter_about(streams_of[11], (D,), 0.5, 4.0, ((0, 8),)),
        "out_grad": noise_with(streams_of[12], (TOKENS, D), 1.0, 6.0, ((0, 32),), (0, 1, 32, 2.75)),
    }


EPS = 1e-05
HIGH = lax.Precision.HIGHEST

@jax.custom_vjp
def low(v):
    return lax.optimization_barrier(v.astype(jnp.bfloat16)).astype(jnp.float32)

@jax.custom_vjp
def low_back(v):
    return v

def low_keep(v):
    return (low(v), None)

def low_pass(kept, grad):
    return (grad,)

def back_keep(v):
    return (v, None)

def back_low(kept, grad):
    return (low(grad),)
low.defvjp(low_keep, low_pass)
low_back.defvjp(back_keep, back_low)

def norm_rows(values, gain, shift):
    centre = lax.optimization_barrier(jnp.mean(values, axis=-1, keepdims=True))
    centred = values - centre
    spread = lax.optimization_barrier(jnp.mean(centred * centred, axis=-1, keepdims=True))
    return centred * lax.rsqrt(spread + EPS) * gain + shift

def all_slopes():
    return 2.0 ** (-8.0 * (jnp.arange(H).astype(jnp.float32) + 1.0) / H)

def attend_sequence(item):
    query, keys, values, seg = item
    scores = jnp.einsum('qhd,khd->hqk', query, keys, precision=HIGH) * HD ** (-0.5)
    place = jnp.arange(SEQ_LEN)
    distance = (place[:, None] - place[None, :]).astype(jnp.float32)
    scores = scores - all_slopes()[:, None, None] * distance[None]
    scores = low_back(scores)
    allowed = (seg[:, None] == seg[None, :]) & (place[None, :] <= place[:, None])
    scores = jnp.where(allowed[None], scores, -1e+30)
    top = lax.optimization_barrier(jnp.max(scores, axis=-1, keepdims=True))
    weights = jnp.exp(scores - top)
    probs = weights / lax.optimization_barrier(jnp.sum(weights, axis=-1, keepdims=True))
    return jnp.einsum('hqk,khd->qhd', low(probs), values, precision=HIGH)

def forward(tokens, norm_gains, norm_biases, qkv_weight, qv_bias, out_weight, out_bias, up_weight, up_bias, down_weight, down_bias, segments):
    normed = low(norm_rows(tokens, norm_gains[0], norm_biases[0]))
    mixed = jnp.dot(normed, qkv_weight.reshape(D, 3 * D), precision=HIGH).reshape(-1, 3, D)
    query = low(low_back(mixed[:, 0] + qv_bias[:, :HD].reshape(D)))
    keys = low(low_back(mixed[:, 1]))
    values = low(low_back(mixed[:, 2] + qv_bias[:, HD:].reshape(D)))
    count = tokens.shape[0] // SEQ_LEN
    shaped = (query.reshape(count, SEQ_LEN, H, HD), keys.reshape(count, SEQ_LEN, H, HD), values.reshape(count, SEQ_LEN, H, HD), segments.reshape(count, SEQ_LEN))
    heads = lax.map(jax.checkpoint(attend_sequence), shaped)
    heads = low(low_back(heads.reshape(-1, D)))
    branch = low_back(jnp.dot(heads, out_weight, precision=HIGH) + out_bias)
    middle = tokens + branch
    normed_mid = low(norm_rows(middle, norm_gains[1], norm_biases[1]))
    inner = low_back(jnp.dot(normed_mid, up_weight, precision=HIGH) + up_bias.reshape(FF))
    active = low(jax.nn.gelu(inner, approximate=True))
    result = low_back(jnp.dot(active, down_weight, precision=HIGH) + down_bias)
    return middle + result

def reference(tokens, segments, norm_gains, norm_biases, qkv_weight, qv_bias, out_weight, out_bias, up_weight, up_bias, down_weight, down_bias, out_grad):
    floats = (tokens.astype(jnp.float32), norm_gains.astype(jnp.float32), norm_biases.astype(jnp.float32), qkv_weight.astype(jnp.float32), qv_bias.astype(jnp.float32), out_weight.astype(jnp.float32), out_bias.astype(jnp.float32), up_weight.astype(jnp.float32), up_bias.astype(jnp.float32), down_weight.astype(jnp.float32), down_bias.astype(jnp.float32))

    def run(*params):
        return forward(*params, segments)
    output, pull = jax.vjp(run, *floats)
    grads = pull(out_grad.astype(jnp.float32))
    return (output.astype(jnp.bfloat16), grads[0], grads[1], grads[2], grads[3], grads[4], grads[5], grads[6], grads[7], grads[8], grads[9], grads[10])
```

```python
import jax
import jax.numpy as jnp
from jax import lax
from jax.experimental import pallas as pl
from jax.experimental.pallas import tpu as pltpu
from jax.sharding import PartitionSpec as P

D = 1024
H = 16
HD = 64
BLOCK = 256
LOG2E = 1.4426950408889634
EPS = 1e-05
F32 = jnp.float32
LOW = jnp.bfloat16


def norm_rows(values, gain, shift):
    centre = jnp.mean(values, axis=-1, keepdims=True)
    centred = values - centre
    spread = jnp.mean(centred * centred, axis=-1, keepdims=True)
    return centred * lax.rsqrt(spread + EPS) * gain + shift


def standard_rows(values):
    centre = jnp.mean(values, axis=-1, keepdims=True)
    centred = values - centre
    spread = jnp.mean(centred * centred, axis=-1, keepdims=True)
    return centred * lax.rsqrt(spread + EPS)


def dot(left, right, left_dim, right_dim):
    return lax.dot_general(
        left, right, (((left_dim,), (right_dim,)), ((), ())), preferred_element_type=F32
    )


def swap(value, bit, size):
    return lax.ppermute(value, "tensor", [(place, place ^ bit) for place in range(size)])


def gather_blocks(own, size):
    blocks = [own]
    if size == 4:
        far = swap(own, 2, size)
        near = swap(own, 1, size)
        return [own, near, far, swap(far, 1, size)]
    for bit in range(1, size):
        blocks.append(swap(own, bit, size))
    return blocks


def spread_blocks(term, size):
    if size == 4:
        across = swap(term(3).astype(LOW), 1, size)
        partner = term(2) + across.astype(F32)
        partner = swap(partner.astype(LOW), 2, size)
        beside = swap(term(1).astype(LOW), 1, size)
        return term(0) + beside.astype(F32) + partner.astype(F32)
    total = term(0)
    for bit in range(1, size):
        total = total + swap(term(bit).astype(LOW), bit, size).astype(F32)
    return total


def column_of(index):
    return slice(index * HD, (index + 1) * HD)


def tile_mask(iota, start_row, place_row, offset):
    return (iota >= start_row - offset) & (iota <= place_row - offset)


def forward_kernel(first_ref, clear_ref, phys_ref, slope_ref, start_ref, q_ref, k_ref, v_ref,
                   out_ref, lse_ref, vt_ref, bias_ref):
    i = pl.program_id(0)
    heads = q_ref.shape[1] // HD
    count = q_ref.shape[0] // BLOCK
    tile = (BLOCK, BLOCK)

    @pl.when(i == 0)
    def _():
        rows = lax.broadcasted_iota(jnp.int32, tile, 0).astype(F32)
        for h in range(heads):
            bias_ref[h] = rows * slope_ref[h]
        for b in range(count):
            block = v_ref[b * BLOCK : (b + 1) * BLOCK, :].astype(F32)
            vt_ref[b] = block.T.astype(LOW)

    here = pl.multiple_of(phys_ref[i] * BLOCK, BLOCK)
    q_block = q_ref[pl.ds(here, BLOCK), :]
    start_row = start_ref[i]
    place_row = i * BLOCK + lax.broadcasted_iota(jnp.int32, (1, BLOCK), 1)
    iota = lax.broadcasted_iota(jnp.int32, tile, 0)

    def step(masked, j, carry):
        there = pl.multiple_of(phys_ref[j] * BLOCK, BLOCK)
        k_block = k_ref[pl.ds(there, BLOCK), :]
        vt_block = vt_ref[phys_ref[j]]
        distance = ((j - i) * BLOCK).astype(F32)
        if masked:
            allowed = tile_mask(iota, start_row, place_row, j * BLOCK)
        result = []
        for h in range(heads):
            top, total, acc = carry[h]
            s = dot(k_block[:, column_of(h)], q_block[:, column_of(h)], 1, 1)
            s = s * (HD**-0.5 * LOG2E) + bias_ref[h]
            if masked:
                s = jnp.where(allowed, s, -1e30)
            off = slope_ref[h] * distance
            new_top = jnp.maximum(top, jnp.max(s, axis=0, keepdims=True) + off)
            p = jnp.exp2(s - (new_top - off))
            keep = jnp.exp2(top - new_top)
            total = total * keep + jnp.sum(p, axis=0, keepdims=True)
            acc = acc * keep + dot(vt_block[column_of(h), :], p.astype(LOW), 1, 0)
            result.append((new_top, total, acc))
        return tuple(result)

    carry = tuple(
        (
            jnp.full((1, BLOCK), -1e30, F32),
            jnp.zeros((1, BLOCK), F32),
            jnp.zeros((HD, BLOCK), F32),
        )
        for _ in range(heads)
    )
    carry = lax.fori_loop(first_ref[i], clear_ref[i], lambda j, c: step(True, j, c), carry)
    carry = lax.fori_loop(clear_ref[i], i, lambda j, c: step(False, j, c), carry)
    carry = step(True, i, carry)
    lse_ref[i] = jnp.concatenate([top + jnp.log2(total) for top, total, _ in carry], axis=0)
    flat = jnp.concatenate([acc / total for _, total, acc in carry], axis=0)
    out_ref[pl.ds(here, BLOCK), :] = flat.T.astype(LOW)


def backward_kernel(first_ref, clear_ref, phys_ref, slope_ref, start_ref, q_ref, k_ref, v_ref,
                    out_ref, grad_ref, lse_ref, dq_ref, dk_ref, dv_ref,
                    kt_ref, bias_ref, dk_sum, dv_sum):
    i = pl.program_id(0)
    heads = q_ref.shape[1] // HD
    count = q_ref.shape[0] // BLOCK
    tile = (BLOCK, BLOCK)

    @pl.when(i == 0)
    def _():
        rows = lax.broadcasted_iota(jnp.int32, tile, 0).astype(F32)
        for h in range(heads):
            bias_ref[h] = rows * slope_ref[h]
        for b in range(count):
            block = k_ref[b * BLOCK : (b + 1) * BLOCK, :].astype(F32)
            kt_ref[b] = block.T.astype(LOW)
        dk_sum[...] = jnp.zeros_like(dk_sum)
        dv_sum[...] = jnp.zeros_like(dv_sum)

    here = pl.multiple_of(phys_ref[i] * BLOCK, BLOCK)
    q_block = q_ref[pl.ds(here, BLOCK), :]
    g_block = grad_ref[pl.ds(here, BLOCK), :]
    product = (g_block.astype(F32) * out_ref[pl.ds(here, BLOCK), :].astype(F32)).T
    start_row = start_ref[i]
    place_row = i * BLOCK + lax.broadcasted_iota(jnp.int32, (1, BLOCK), 1)
    iota = lax.broadcasted_iota(jnp.int32, tile, 0)
    lse = lse_ref[i]
    inner = [jnp.sum(product[column_of(h), :], axis=0, keepdims=True) for h in range(heads)]

    def step(masked, j, carry):
        rows = pl.ds(pl.multiple_of(phys_ref[j] * BLOCK, BLOCK), BLOCK)
        k_block = k_ref[rows, :]
        v_block = v_ref[rows, :]
        kt_block = kt_ref[phys_ref[j]]
        distance = ((j - i) * BLOCK).astype(F32)
        if masked:
            allowed = tile_mask(iota, start_row, place_row, j * BLOCK)
        result = []
        for h in range(heads):
            s = dot(k_block[:, column_of(h)], q_block[:, column_of(h)], 1, 1)
            s = s * (HD**-0.5 * LOG2E) + bias_ref[h]
            p = jnp.exp2(s - (lse[h : h + 1, :] - slope_ref[h] * distance))
            if masked:
                p = jnp.where(allowed, p, 0.0)
            dp = dot(v_block[:, column_of(h)], g_block[:, column_of(h)], 1, 1)
            ds = (p * (dp - inner[h])).astype(LOW)
            dv_sum[h, rows, :] += dot(p.astype(LOW), g_block[:, column_of(h)], 1, 0)
            dk_sum[h, rows, :] += dot(ds, q_block[:, column_of(h)], 1, 0)
            result.append(carry[h] + dot(kt_block[column_of(h), :], ds, 1, 0))
        return tuple(result)

    carry = tuple(jnp.zeros((HD, BLOCK), F32) for _ in range(heads))
    carry = lax.fori_loop(first_ref[i], clear_ref[i], lambda j, c: step(True, j, c), carry)
    carry = lax.fori_loop(clear_ref[i], i, lambda j, c: step(False, j, c), carry)
    carry = step(True, i, carry)
    flat = jnp.concatenate(carry, axis=0) * HD**-0.5
    dq_ref[pl.ds(here, BLOCK), :] = flat.T.astype(LOW)

    @pl.when(i == count - 1)
    def _():
        for b in range(count):
            rows = slice(b * BLOCK, (b + 1) * BLOCK)
            dk_ref[rows, :] = (
                jnp.concatenate([dk_sum[h, rows, :] for h in range(heads)], axis=1) * HD**-0.5
            ).astype(LOW)
            dv_ref[rows, :] = jnp.concatenate(
                [dv_sum[h, rows, :] for h in range(heads)], axis=1
            ).astype(LOW)


SMEM = pl.BlockSpec(memory_space=pltpu.SMEM)
VMEM = pl.BlockSpec(memory_space=pltpu.VMEM)
LIMIT = 48 * 1024 * 1024


def attend_forward(plan, query, keys, values):
    total, width = query.shape
    heads, count = width // HD, total // BLOCK
    return pl.pallas_call(
        forward_kernel,
        grid=(count,),
        out_shape=(
            jax.ShapeDtypeStruct((total, width), LOW),
            jax.ShapeDtypeStruct((count, heads, BLOCK), F32),
        ),
        in_specs=[SMEM] * 4 + [VMEM] * 4,
        out_specs=(VMEM, VMEM),
        scratch_shapes=[
            pltpu.VMEM((count, width, BLOCK), LOW),
            pltpu.VMEM((heads, BLOCK, BLOCK), F32),
        ],
        compiler_params=pltpu.CompilerParams(vmem_limit_bytes=LIMIT),
        cost_estimate=pl.CostEstimate(
            flops=2 * total * total * width, bytes_accessed=8 * total * width,
            transcendentals=total * total * heads // 2),
        name="attend_forward",
    )(*plan, query, keys, values)


def attend_backward(plan, query, keys, values, heads_out, heads_grad, lse):
    total, width = query.shape
    heads, count = width // HD, total // BLOCK
    return pl.pallas_call(
        backward_kernel,
        grid=(count,),
        out_shape=(jax.ShapeDtypeStruct((total, width), LOW),) * 3,
        in_specs=[SMEM] * 4 + [VMEM] * 7,
        out_specs=(VMEM,) * 3,
        scratch_shapes=[
            pltpu.VMEM((count, width, BLOCK), LOW),
            pltpu.VMEM((heads, BLOCK, BLOCK), F32),
            pltpu.VMEM((heads, total, HD), F32),
            pltpu.VMEM((heads, total, HD), F32),
        ],
        compiler_params=pltpu.CompilerParams(vmem_limit_bytes=LIMIT),
        cost_estimate=pl.CostEstimate(
            flops=5 * total * total * width, bytes_accessed=16 * total * width,
            transcendentals=total * total * heads // 2),
        name="attend_backward",
    )(*plan, query, keys, values, heads_out, heads_grad, lse)


def attention_plan(segments, position, size, local_heads):
    total = segments.shape[0]
    count = total // BLOCK
    group = total // size // BLOCK
    place = jnp.arange(total, dtype=jnp.int32)
    fresh = jnp.concatenate([jnp.ones((1,), bool), segments[1:] != segments[:-1]])
    starts = lax.cummax(jnp.where(fresh, place, 0))
    block = jnp.arange(count, dtype=jnp.int32)
    first = starts[::BLOCK] // BLOCK
    clear = (starts[BLOCK - 1 :: BLOCK] + (BLOCK - 1)) // BLOCK
    clear = jnp.clip(clear, first, block)
    phys = ((block // group) ^ position) * group + block % group
    index = position * local_heads + jnp.arange(local_heads)
    slopes = 2.0 ** (-8.0 * (index.astype(F32) + 1.0) / H) * LOG2E
    return (first, clear, phys, slopes, starts.reshape(count, 1, BLOCK))


def on_device(tensor_size, dp_size):
    def run(tokens, segments, norm_gains, norm_biases, qkv_weight, qv_bias, out_weight, out_bias,
            up_weight, up_bias, down_weight, down_bias, out_grad):
        size = tensor_size
        position = lax.axis_index("tensor")
        part = D // dp_size
        local_width = qkv_weight.shape[2]
        local_heads = local_width // HD
        width = 3 * local_width

        token_blocks = gather_blocks(tokens, size)

        pieces = [norm_gains.reshape(-1), norm_biases.reshape(-1), out_bias, down_bias,
                  qv_bias.reshape(-1), up_bias.reshape(-1)]
        small = jnp.concatenate(pieces)
        extra = -(-small.shape[0] // (16 * width)) * 16
        small = jnp.pad(small, (0, extra * width - small.shape[0])).reshape(extra, width)
        packed = jnp.concatenate([qkv_weight.reshape(part, width), small], axis=0)
        packed = lax.all_gather(packed, "dp", axis=0)
        qkv_full = packed[:, :part].reshape(D, width)
        small = packed[:, part:].reshape(dp_size, -1)
        full = []
        place = 0
        for piece, shape in zip(
            pieces,
            (norm_gains.shape, norm_biases.shape, (1, part), (1, part), qv_bias.shape, up_bias.shape),
        ):
            block = small[:, place : place + piece.size].reshape((dp_size,) + shape)
            full.append(block.transpose(1, 0, 2).reshape(shape[0], -1).astype(F32))
            place += piece.size
        gain_rows, shift_rows, out_shift, down_shift, qv_full, up_shift = full
        out_full = lax.all_gather(out_weight, "dp", axis=1, tiled=True)
        up_full = lax.all_gather(up_weight, "dp", axis=0, tiled=True)
        down_full = lax.all_gather(down_weight, "dp", axis=1, tiled=True)
        grad_blocks = gather_blocks(out_grad, size)

        plan = attention_plan(segments, position, size, local_heads)
        inputs = tokens.astype(F32)
        normed = jnp.concatenate(
            [norm_rows(b.astype(F32), gain_rows[0], shift_rows[0]).astype(LOW)
             for b in token_blocks]
        )
        mixed_bias = jnp.concatenate(
            [qv_full[:, :HD].reshape(-1), jnp.zeros((local_width,), F32),
             qv_full[:, HD:].reshape(-1)]
        )
        mixed = (dot(normed, qkv_full, 1, 0) + mixed_bias).astype(LOW)
        query, keys, values = (
            mixed[:, c * local_width : (c + 1) * local_width] for c in range(3)
        )
        heads, lse = attend_forward(plan, query, keys, values)
        rows = tokens.shape[0]

        def block_of(array, r):
            return array[r * rows : (r + 1) * rows]

        projected = spread_blocks(lambda r: dot(block_of(heads, r), out_full, 1, 0), size)
        middle = inputs + projected + out_shift
        normed_mid = norm_rows(middle, gain_rows[1], shift_rows[1]).astype(LOW)
        mid_blocks = gather_blocks(normed_mid, size)

        active, inner_grad = [], []
        for r in range(size):
            inner = dot(mid_blocks[r], up_full, 1, 0) + up_shift.reshape(-1)
            value, pull = jax.vjp(lambda u: jax.nn.gelu(u, approximate=True), inner)
            active.append(value.astype(LOW))
            inner_grad.append(pull(dot(grad_blocks[r], down_full, 1, 1))[0].astype(LOW))
        mid_norm_grad = spread_blocks(lambda r: dot(inner_grad[r], up_full, 1, 1), size)
        middle_back, gain_mid, shift_mid = jax.vjp(
            norm_rows, middle, gain_rows[1], shift_rows[1]
        )[1](mid_norm_grad)
        middle_grad = out_grad.astype(F32) + middle_back
        middle_low = middle_grad.astype(LOW)
        middle_blocks = gather_blocks(middle_low, size)

        branch = spread_blocks(lambda r: dot(active[r], down_full, 1, 0), size)
        output = (middle + branch + down_shift).astype(LOW)

        active = jnp.concatenate(active)
        inner_grad = jnp.concatenate(inner_grad)
        up_grad = dot(jnp.concatenate(mid_blocks), inner_grad, 0, 0).astype(LOW)
        down_grad = dot(active, jnp.concatenate(grad_blocks), 0, 0).astype(LOW)
        up_sum = lax.psum_scatter(up_grad, "dp", scatter_dimension=0, tiled=True).astype(F32)
        down_sum = lax.psum_scatter(down_grad, "dp", scatter_dimension=1, tiled=True).astype(F32)
        up_shift_grad = jnp.sum(inner_grad, axis=0, dtype=F32).reshape(up_bias.shape[0], -1)
        down_shift_grad = jnp.sum(out_grad, axis=0, dtype=F32)

        middle_all = jnp.concatenate(middle_blocks)
        heads_grad = jnp.concatenate(
            [dot(b, out_full, 1, 1).astype(LOW) for b in middle_blocks]
        )
        out_shift_grad = jnp.sum(middle_low, axis=0, dtype=F32)
        out_weight_grad = dot(heads, middle_all, 0, 0).astype(LOW)
        out_weight_sum = lax.psum_scatter(
            out_weight_grad, "dp", scatter_dimension=1, tiled=True
        ).astype(F32)
        mixed_grads = attend_backward(plan, query, keys, values, heads, heads_grad, lse)
        flat_grad = jnp.concatenate(mixed_grads, axis=1)
        normed_terms = [dot(block_of(flat_grad, r), qkv_full, 1, 1) for r in range(size)]
        normed_grad = spread_blocks(lambda r: normed_terms[r], size)
        qkv_grad = dot(normed, flat_grad, 0, 0).astype(LOW)
        qkv_sum = lax.psum_scatter(qkv_grad, "dp", scatter_dimension=0, tiled=True)
        qkv_sum = qkv_sum.astype(F32).reshape(part, 3, local_width)
        query_sum = jnp.sum(mixed_grads[0], axis=0, dtype=F32).reshape(local_heads, HD)
        value_sum = jnp.sum(mixed_grads[2], axis=0, dtype=F32).reshape(local_heads, HD)
        qv_grad = jnp.concatenate([query_sum, value_sum], axis=1)

        gain_first = sum(
            jnp.sum(term * standard_rows(b.astype(F32)), axis=0)
            for term, b in zip(normed_terms, token_blocks)
        )
        shift_first = sum(jnp.sum(term, axis=0) for term in normed_terms)
        input_back = jax.vjp(lambda v: norm_rows(v, gain_rows[0], shift_rows[0]), inputs)[1](
            normed_grad
        )[0]
        input_grad = middle_grad + input_back

        both = jnp.stack(
            [gain_first, gain_mid, shift_first, shift_mid, out_shift_grad, down_shift_grad]
        )
        both = both.reshape(6, dp_size, part).transpose(1, 0, 2).reshape(dp_size, -1)
        single = [
            g.reshape(g.shape[0], dp_size, -1).transpose(1, 0, 2).reshape(dp_size, -1)
            for g in (qv_grad, up_shift_grad)
        ]
        sums = jnp.concatenate([both] + single, axis=1)
        span = sums.shape[1]
        padded = -(-span // 1024) * 1024
        sums = jnp.pad(sums, ((0, 0), (0, padded - span))).reshape(dp_size * padded // 128, 128)
        sums = lax.psum_scatter(sums, "dp", scatter_dimension=0, tiled=True).reshape(-1)
        across = lax.psum(sums[: 6 * part].reshape(6, part), "tensor")
        qv_sum = sums[6 * part : 6 * part + qv_bias.size].reshape(qv_bias.shape)
        up_shift_sum = sums[6 * part + qv_bias.size : span].reshape(up_bias.shape)
        return (
            output,
            input_grad,
            across[0:2],
            across[2:4],
            qkv_sum,
            qv_sum,
            out_weight_sum,
            across[4],
            up_sum,
            up_shift_sum,
            down_sum,
            across[5],
        )

    return run


def solution(mesh):
    placed = (
        P(("dp", "tensor"), None),
        P("dp"),
        P(None, "dp"),
        P(None, "dp"),
        P("dp", None, "tensor"),
        P("tensor", "dp"),
        P("tensor", "dp"),
        P("dp"),
        P("dp", "tensor"),
        P("tensor", "dp"),
        P("tensor", "dp"),
        P("dp"),
        P(("dp", "tensor"), None),
    )
    return jax.shard_map(
        on_device(mesh.shape["tensor"], mesh.shape["dp"]),
        mesh=mesh,
        in_specs=placed,
        out_specs=(
            P(("dp", "tensor"), None),
            P(("dp", "tensor"), None),
            P(None, "dp"),
            P(None, "dp"),
            P("dp", None, "tensor"),
            P("tensor", "dp"),
            P("tensor", "dp"),
            P("dp"),
            P("dp", "tensor"),
            P("tensor", "dp"),
            P("tensor", "dp"),
            P("dp"),
        ),
        check_vma=False,
    )
```

```python
import jax
import jax.numpy as jnp
from jax import lax
from jax.experimental import pallas as pl
from jax.experimental.pallas import tpu as pltpu
from jax.sharding import PartitionSpec as P

D = 1024
H = 16
HD = 64
BLOCK = 256
LOG2E = 1.4426950408889634
EPS = 1e-05
F32 = jnp.float32
LOW = jnp.bfloat16


def norm_rows(values, gain, shift):
    centre = jnp.mean(values, axis=-1, keepdims=True)
    centred = values - centre
    spread = jnp.mean(centred * centred, axis=-1, keepdims=True)
    return centred * lax.rsqrt(spread + EPS) * gain + shift


def standard_rows(values):
    centre = jnp.mean(values, axis=-1, keepdims=True)
    centred = values - centre
    spread = jnp.mean(centred * centred, axis=-1, keepdims=True)
    return centred * lax.rsqrt(spread + EPS)


def dot(left, right, left_dim, right_dim):
    return lax.dot_general(
        left, right, (((left_dim,), (right_dim,)), ((), ())), preferred_element_type=F32
    )


def swap(value, bit, size):
    return lax.ppermute(value, "tensor", [(place, place ^ bit) for place in range(size)])


def gather_blocks(own, size):
    blocks = [own]
    if size == 4:
        far = swap(own, 2, size)
        near = swap(own, 1, size)
        return [own, near, far, swap(far, 1, size)]
    for bit in range(1, size):
        blocks.append(swap(own, bit, size))
    return blocks


def spread_blocks(term, size, later=None):
    if later is not None:
        if size == 4:
            across, later = lax.optimization_barrier((swap(term(3).astype(LOW), 1, size), later))
            return spread_after(term, size, across), later
        return spread_blocks(term, size), later
    if size == 4:
        return spread_after(term, size, swap(term(3).astype(LOW), 1, size))
    total = term(0)
    for bit in range(1, size):
        total = total + swap(term(bit).astype(LOW), bit, size).astype(F32)
    return total


def spread_after(term, size, across):
    partner = term(2) + across.astype(F32)
    partner = swap(partner.astype(LOW), 2, size)
    beside = swap(term(1).astype(LOW), 1, size)
    return term(0) + beside.astype(F32) + partner.astype(F32)


def column_of(index):
    return slice(index * HD, (index + 1) * HD)


def tile_mask(iota, start_row, place_row, offset):
    return (iota >= start_row - offset) & (iota <= place_row - offset)


def forward_kernel(first_ref, clear_ref, phys_ref, slope_ref, start_ref, q_ref, k_ref, v_ref,
                   out_ref, lse_ref, vt_ref, bias_ref):
    i = pl.program_id(0)
    heads = q_ref.shape[1] // HD
    count = q_ref.shape[0] // BLOCK
    tile = (BLOCK, BLOCK)

    @pl.when(i == 0)
    def _():
        rows = lax.broadcasted_iota(jnp.int32, tile, 0).astype(F32)
        for h in range(heads):
            bias_ref[h] = rows * slope_ref[h]
        for b in range(count):
            block = v_ref[b * BLOCK : (b + 1) * BLOCK, :].astype(F32)
            vt_ref[b] = block.T.astype(LOW)

    here = pl.multiple_of(phys_ref[i] * BLOCK, BLOCK)
    q_block = q_ref[pl.ds(here, BLOCK), :]
    start_row = start_ref[i]
    place_row = i * BLOCK + lax.broadcasted_iota(jnp.int32, (1, BLOCK), 1)
    iota = lax.broadcasted_iota(jnp.int32, tile, 0)

    def step(masked, j, carry):
        there = pl.multiple_of(phys_ref[j] * BLOCK, BLOCK)
        k_block = k_ref[pl.ds(there, BLOCK), :]
        vt_block = vt_ref[phys_ref[j]]
        distance = ((j - i) * BLOCK).astype(F32)
        if masked:
            allowed = tile_mask(iota, start_row, place_row, j * BLOCK)
        result = []
        for h in range(heads):
            top, total, acc = carry[h]
            s = dot(k_block[:, column_of(h)], q_block[:, column_of(h)], 1, 1)
            s = s * (HD**-0.5 * LOG2E) + bias_ref[h]
            if masked:
                s = jnp.where(allowed, s, -1e30)
            off = slope_ref[h] * distance
            new_top = jnp.maximum(top, jnp.max(s, axis=0, keepdims=True) + off)
            p = jnp.exp2(s - (new_top - off))
            keep = jnp.exp2(top - new_top)
            total = total * keep + jnp.sum(p, axis=0, keepdims=True)
            acc = acc * keep + dot(vt_block[column_of(h), :], p.astype(LOW), 1, 0)
            result.append((new_top, total, acc))
        return tuple(result)

    carry = tuple(
        (
            jnp.full((1, BLOCK), -1e30, F32),
            jnp.zeros((1, BLOCK), F32),
            jnp.zeros((HD, BLOCK), F32),
        )
        for _ in range(heads)
    )
    carry = lax.fori_loop(first_ref[i], clear_ref[i], lambda j, c: step(True, j, c), carry)
    carry = lax.fori_loop(clear_ref[i], i, lambda j, c: step(False, j, c), carry)
    carry = step(True, i, carry)
    lse_ref[i] = jnp.concatenate([top + jnp.log2(total) for top, total, _ in carry], axis=0)
    flat = jnp.concatenate([acc / total for _, total, acc in carry], axis=0)
    out_ref[pl.ds(here, BLOCK), :] = flat.T.astype(LOW)


def backward_kernel(first_ref, clear_ref, phys_ref, slope_ref, start_ref, q_ref, k_ref, v_ref,
                    out_ref, grad_ref, lse_ref, dq_ref, dk_ref, dv_ref,
                    kt_ref, bias_ref, dk_sum, dv_sum):
    i = pl.program_id(0)
    heads = q_ref.shape[1] // HD
    count = q_ref.shape[0] // BLOCK
    tile = (BLOCK, BLOCK)

    @pl.when(i == 0)
    def _():
        rows = lax.broadcasted_iota(jnp.int32, tile, 0).astype(F32)
        for h in range(heads):
            bias_ref[h] = rows * slope_ref[h]
        for b in range(count):
            block = k_ref[b * BLOCK : (b + 1) * BLOCK, :].astype(F32)
            kt_ref[b] = block.T.astype(LOW)
        dk_sum[...] = jnp.zeros_like(dk_sum)
        dv_sum[...] = jnp.zeros_like(dv_sum)

    here = pl.multiple_of(phys_ref[i] * BLOCK, BLOCK)
    q_block = q_ref[pl.ds(here, BLOCK), :]
    g_block = grad_ref[pl.ds(here, BLOCK), :]
    product = (g_block.astype(F32) * out_ref[pl.ds(here, BLOCK), :].astype(F32)).T
    start_row = start_ref[i]
    place_row = i * BLOCK + lax.broadcasted_iota(jnp.int32, (1, BLOCK), 1)
    iota = lax.broadcasted_iota(jnp.int32, tile, 0)
    lse = lse_ref[i]
    inner = [jnp.sum(product[column_of(h), :], axis=0, keepdims=True) for h in range(heads)]

    def step(masked, j, carry):
        rows = pl.ds(pl.multiple_of(phys_ref[j] * BLOCK, BLOCK), BLOCK)
        k_block = k_ref[rows, :]
        v_block = v_ref[rows, :]
        kt_block = kt_ref[phys_ref[j]]
        distance = ((j - i) * BLOCK).astype(F32)
        if masked:
            allowed = tile_mask(iota, start_row, place_row, j * BLOCK)
        result = []
        for h in range(heads):
            s = dot(k_block[:, column_of(h)], q_block[:, column_of(h)], 1, 1)
            s = s * (HD**-0.5 * LOG2E) + bias_ref[h]
            p = jnp.exp2(s - (lse[h : h + 1, :] - slope_ref[h] * distance))
            if masked:
                p = jnp.where(allowed, p, 0.0)
            dp = dot(v_block[:, column_of(h)], g_block[:, column_of(h)], 1, 1)
            ds = (p * (dp - inner[h])).astype(LOW)
            dv_sum[h, rows, :] += dot(p.astype(LOW), g_block[:, column_of(h)], 1, 0)
            dk_sum[h, rows, :] += dot(ds, q_block[:, column_of(h)], 1, 0)
            result.append(carry[h] + dot(kt_block[column_of(h), :], ds, 1, 0))
        return tuple(result)

    carry = tuple(jnp.zeros((HD, BLOCK), F32) for _ in range(heads))
    carry = lax.fori_loop(first_ref[i], clear_ref[i], lambda j, c: step(True, j, c), carry)
    carry = lax.fori_loop(clear_ref[i], i, lambda j, c: step(False, j, c), carry)
    carry = step(True, i, carry)
    flat = jnp.concatenate(carry, axis=0) * HD**-0.5
    dq_ref[pl.ds(here, BLOCK), :] = flat.T.astype(LOW)

    @pl.when(i == count - 1)
    def _():
        for b in range(count):
            rows = slice(b * BLOCK, (b + 1) * BLOCK)
            dk_ref[rows, :] = (
                jnp.concatenate([dk_sum[h, rows, :] for h in range(heads)], axis=1) * HD**-0.5
            ).astype(LOW)
            dv_ref[rows, :] = jnp.concatenate(
                [dv_sum[h, rows, :] for h in range(heads)], axis=1
            ).astype(LOW)


SMEM = pl.BlockSpec(memory_space=pltpu.SMEM)
VMEM = pl.BlockSpec(memory_space=pltpu.VMEM)
LIMIT = 48 * 1024 * 1024


def attend_forward(plan, query, keys, values):
    total, width = query.shape
    heads, count = width // HD, total // BLOCK
    return pl.pallas_call(
        forward_kernel,
        grid=(count,),
        out_shape=(
            jax.ShapeDtypeStruct((total, width), LOW),
            jax.ShapeDtypeStruct((count, heads, BLOCK), F32),
        ),
        in_specs=[SMEM] * 4 + [VMEM] * 4,
        out_specs=(VMEM, VMEM),
        scratch_shapes=[
            pltpu.VMEM((count, width, BLOCK), LOW),
            pltpu.VMEM((heads, BLOCK, BLOCK), F32),
        ],
        compiler_params=pltpu.CompilerParams(vmem_limit_bytes=LIMIT),
        cost_estimate=pl.CostEstimate(
            flops=2 * total * total * width, bytes_accessed=8 * total * width,
            transcendentals=total * total * heads // 2),
        name="attend_forward",
    )(*plan, query, keys, values)


def attend_backward(plan, query, keys, values, heads_out, heads_grad, lse):
    total, width = query.shape
    heads, count = width // HD, total // BLOCK
    return pl.pallas_call(
        backward_kernel,
        grid=(count,),
        out_shape=(jax.ShapeDtypeStruct((total, width), LOW),) * 3,
        in_specs=[SMEM] * 4 + [VMEM] * 7,
        out_specs=(VMEM,) * 3,
        scratch_shapes=[
            pltpu.VMEM((count, width, BLOCK), LOW),
            pltpu.VMEM((heads, BLOCK, BLOCK), F32),
            pltpu.VMEM((heads, total, HD), F32),
            pltpu.VMEM((heads, total, HD), F32),
        ],
        compiler_params=pltpu.CompilerParams(vmem_limit_bytes=LIMIT),
        cost_estimate=pl.CostEstimate(
            flops=5 * total * total * width, bytes_accessed=16 * total * width,
            transcendentals=total * total * heads // 2),
        name="attend_backward",
    )(*plan, query, keys, values, heads_out, heads_grad, lse)


def attention_plan(segments, position, size, local_heads):
    total = segments.shape[0]
    count = total // BLOCK
    group = total // size // BLOCK
    place = jnp.arange(total, dtype=jnp.int32)
    fresh = jnp.concatenate([jnp.ones((1,), bool), segments[1:] != segments[:-1]])
    starts = lax.cummax(jnp.where(fresh, place, 0))
    block = jnp.arange(count, dtype=jnp.int32)
    first = starts[::BLOCK] // BLOCK
    clear = (starts[BLOCK - 1 :: BLOCK] + (BLOCK - 1)) // BLOCK
    clear = jnp.clip(clear, first, block)
    phys = ((block // group) ^ position) * group + block % group
    index = position * local_heads + jnp.arange(local_heads)
    slopes = 2.0 ** (-8.0 * (index.astype(F32) + 1.0) / H) * LOG2E
    return (first, clear, phys, slopes, starts.reshape(count, 1, BLOCK))


def on_device(tensor_size, dp_size):
    def run(tokens, segments, norm_gains, norm_biases, qkv_weight, qv_bias, out_weight, out_bias,
            up_weight, up_bias, down_weight, down_bias, out_grad):
        size = tensor_size
        position = lax.axis_index("tensor")
        part = D // dp_size
        local_width = qkv_weight.shape[2]
        local_heads = local_width // HD
        width = 3 * local_width

        token_blocks = gather_blocks(tokens, size)

        pieces = [norm_gains.reshape(-1), norm_biases.reshape(-1), out_bias, down_bias,
                  qv_bias.reshape(-1), up_bias.reshape(-1)]
        small = jnp.concatenate(pieces)
        wide = width + local_width
        extra = -(-small.shape[0] // (16 * wide)) * 16
        small = jnp.pad(small, (0, extra * wide - small.shape[0])).reshape(extra, wide)
        packed = jnp.concatenate([qkv_weight.reshape(part, width), out_weight.T], axis=1)
        packed = jnp.concatenate([packed, small], axis=0)
        packed = lax.all_gather(packed, "dp", axis=0)
        attention_full = packed[:, :part].reshape(D, wide)
        qkv_full = attention_full[:, :width]
        out_full = attention_full[:, width:]
        small = packed[:, part:].reshape(dp_size, -1)
        full = []
        place = 0
        for piece, shape in zip(
            pieces,
            (norm_gains.shape, norm_biases.shape, (1, part), (1, part), qv_bias.shape, up_bias.shape),
        ):
            block = small[:, place : place + piece.size].reshape((dp_size,) + shape)
            full.append(block.transpose(1, 0, 2).reshape(shape[0], -1).astype(F32))
            place += piece.size
        gain_rows, shift_rows, out_shift, down_shift, qv_full, up_shift = full
        units = up_weight.shape[1]
        mlp_full = lax.all_gather(
            jnp.concatenate([up_weight, down_weight.T], axis=1), "dp", axis=0, tiled=True
        )
        up_full = mlp_full[:, :units]
        down_full = mlp_full[:, units:]
        grad_blocks = gather_blocks(out_grad, size)

        plan = attention_plan(segments, position, size, local_heads)
        inputs = tokens.astype(F32)
        normed = jnp.concatenate(
            [norm_rows(b.astype(F32), gain_rows[0], shift_rows[0]).astype(LOW)
             for b in token_blocks]
        )
        mixed_bias = jnp.concatenate(
            [qv_full[:, :HD].reshape(-1), jnp.zeros((local_width,), F32),
             qv_full[:, HD:].reshape(-1)]
        )
        mixed = (dot(normed, qkv_full, 1, 0) + mixed_bias).astype(LOW)
        query, keys, values = (
            mixed[:, c * local_width : (c + 1) * local_width] for c in range(3)
        )
        heads, lse = attend_forward(plan, query, keys, values)
        rows = tokens.shape[0]

        def block_of(array, r):
            return array[r * rows : (r + 1) * rows]

        projected = spread_blocks(lambda r: dot(block_of(heads, r), out_full, 1, 1), size)
        active_grad = [dot(b, down_full, 1, 0) for b in grad_blocks]
        projected, active_grad = lax.optimization_barrier((projected, active_grad))
        middle = inputs + projected + out_shift
        normed_mid = norm_rows(middle, gain_rows[1], shift_rows[1]).astype(LOW)
        mid_blocks = gather_blocks(normed_mid, size)

        active, inner_grad = [], []
        for r in range(size):
            inner = dot(mid_blocks[r], up_full, 1, 0) + up_shift.reshape(-1)
            value, pull = jax.vjp(lambda u: jax.nn.gelu(u, approximate=True), inner)
            active.append(value.astype(LOW))
            inner_grad.append(pull(active_grad[r])[0].astype(LOW))
        mid_norm_grad, kept_grad = spread_blocks(
            lambda r: dot(inner_grad[r], up_full, 1, 1), size, inner_grad
        )
        middle_back, gain_mid, shift_mid = jax.vjp(
            norm_rows, middle, gain_rows[1], shift_rows[1]
        )[1](mid_norm_grad)
        middle_grad = out_grad.astype(F32) + middle_back
        middle_low = middle_grad.astype(LOW)
        middle_blocks = gather_blocks(middle_low, size)

        kept_active, heads, last = lax.optimization_barrier((active, heads, middle_blocks[-1]))
        middle_blocks = middle_blocks[:-1] + [last]
        branch = spread_blocks(lambda r: dot(kept_active[r], down_full, 1, 1), size)
        output = (middle + branch + down_shift).astype(LOW)

        active = jnp.concatenate(active)
        inner_grad = jnp.concatenate(kept_grad)
        up_grad = dot(jnp.concatenate(mid_blocks), inner_grad, 0, 0).astype(LOW)
        down_grad = dot(jnp.concatenate(grad_blocks), active, 0, 0).astype(LOW)
        mlp_sum = lax.psum_scatter(
            jnp.concatenate([up_grad, down_grad], axis=1), "dp", scatter_dimension=0, tiled=True
        ).astype(F32)
        up_sum = mlp_sum[:, :units]
        down_sum = mlp_sum[:, units:].T
        up_shift_grad = jnp.sum(inner_grad, axis=0, dtype=F32).reshape(up_bias.shape[0], -1)
        down_shift_grad = jnp.sum(out_grad, axis=0, dtype=F32)

        middle_all = jnp.concatenate(middle_blocks)
        heads_grad = jnp.concatenate(
            [dot(b, out_full, 1, 0).astype(LOW) for b in middle_blocks]
        )
        out_shift_grad = jnp.sum(middle_low, axis=0, dtype=F32)
        out_weight_grad = dot(middle_all, heads, 0, 0).astype(LOW)
        mixed_grads = attend_backward(plan, query, keys, values, heads, heads_grad, lse)
        flat_grad = jnp.concatenate(mixed_grads, axis=1)
        normed_terms = [dot(block_of(flat_grad, r), qkv_full, 1, 1) for r in range(size)]
        normed_grad = spread_blocks(lambda r: normed_terms[r], size)
        qkv_grad = dot(normed, flat_grad, 0, 0).astype(LOW)
        attention_sum = lax.psum_scatter(
            jnp.concatenate([qkv_grad, out_weight_grad], axis=1),
            "dp", scatter_dimension=0, tiled=True,
        ).astype(F32)
        qkv_sum = attention_sum[:, :width].reshape(part, 3, local_width)
        out_weight_sum = attention_sum[:, width:].T
        query_sum = jnp.sum(mixed_grads[0], axis=0, dtype=F32).reshape(local_heads, HD)
        value_sum = jnp.sum(mixed_grads[2], axis=0, dtype=F32).reshape(local_heads, HD)
        qv_grad = jnp.concatenate([query_sum, value_sum], axis=1)

        gain_first = sum(
            jnp.sum(term * standard_rows(b.astype(F32)), axis=0)
            for term, b in zip(normed_terms, token_blocks)
        )
        shift_first = sum(jnp.sum(term, axis=0) for term in normed_terms)
        input_back = jax.vjp(lambda v: norm_rows(v, gain_rows[0], shift_rows[0]), inputs)[1](
            normed_grad
        )[0]
        input_grad = middle_grad + input_back

        both = jnp.stack(
            [gain_first, gain_mid, shift_first, shift_mid, out_shift_grad, down_shift_grad]
        )
        both = both.reshape(6, dp_size, part).transpose(1, 0, 2).reshape(dp_size, -1)
        single = [
            g.reshape(g.shape[0], dp_size, -1).transpose(1, 0, 2).reshape(dp_size, -1)
            for g in (qv_grad, up_shift_grad)
        ]
        sums = jnp.concatenate([both] + single, axis=1)
        span = sums.shape[1]
        padded = -(-span // 1024) * 1024
        sums = jnp.pad(sums, ((0, 0), (0, padded - span))).reshape(dp_size * padded // 128, 128)
        sums = lax.psum_scatter(sums, "dp", scatter_dimension=0, tiled=True).reshape(-1)
        across = lax.psum(sums[: 6 * part].reshape(6, part), "tensor")
        qv_sum = sums[6 * part : 6 * part + qv_bias.size].reshape(qv_bias.shape)
        up_shift_sum = sums[6 * part + qv_bias.size : span].reshape(up_bias.shape)
        return (
            output,
            input_grad,
            across[0:2],
            across[2:4],
            qkv_sum,
            qv_sum,
            out_weight_sum,
            across[4],
            up_sum,
            up_shift_sum,
            down_sum,
            across[5],
        )

    return run


def solution(mesh):
    placed = (
        P(("dp", "tensor"), None),
        P("dp"),
        P(None, "dp"),
        P(None, "dp"),
        P("dp", None, "tensor"),
        P("tensor", "dp"),
        P("tensor", "dp"),
        P("dp"),
        P("dp", "tensor"),
        P("tensor", "dp"),
        P("tensor", "dp"),
        P("dp"),
        P(("dp", "tensor"), None),
    )
    return jax.shard_map(
        on_device(mesh.shape["tensor"], mesh.shape["dp"]),
        mesh=mesh,
        in_specs=placed,
        out_specs=(
            P(("dp", "tensor"), None),
            P(("dp", "tensor"), None),
            P(None, "dp"),
            P(None, "dp"),
            P("dp", None, "tensor"),
            P("tensor", "dp"),
            P("tensor", "dp"),
            P("dp"),
            P("dp", "tensor"),
            P("tensor", "dp"),
            P("tensor", "dp"),
            P("dp"),
        ),
        check_vma=False,
    )
```
